32 devices in a mesh: groups: 2 (over y), shard: 4 (over z), inner: 4 (over x, core).
Axes of the slice: x: 2, y: 2, z: 4, core: 2. Of those that a mesh axis runs over, the one named last changes fastest.
Arguments:
- item_last: bfloat16 [256, 2048], P(('groups', 'shard')), parts along dimension 0, may hold values from -260 to 260, as said below
- adapter: bfloat16 [2048, 4096], P(None, 'inner'), may hold values from -0.125 to 0.125
- user_gain: float32 [4096], replicated, may hold values from 0.5 to 1.5
- w_gate: bfloat16 [4096, 6144], P('shard', 'inner'), may hold values from -0.09375 to 0.09375
- w_up: bfloat16 [4096, 6144], P('shard', 'inner'), may hold values from -0.09375 to 0.09375
- owners: int32 [1024, 1], P(('groups', 'shard')), parts along dimension 0, may hold values from 0 to 3; in each aligned block of 128 rows (0 to 127, 128 to 255, ...) at most 64 rows name the same one
- item_rows: int32 [1024], P(('groups', 'shard')), parts along dimension 0, may hold values from 0 to 31
- lengths: int32 [8], P(('groups', 'shard')), parts along dimension 0, may hold values from 32 to 128
- d_hidden: bfloat16 [1024, 6144], P(('groups', 'shard'), 'inner'), parts along dimension 0, may hold values from -6 to 6
Outputs:
- hidden: bfloat16 [1024, 6144], P(('groups', 'shard'), 'inner'), parts along dimension 0
- item_grad: float32 [256, 4096], P(('groups', 'shard'), 'inner'), parts along dimension 0
The draws below stay inside these ranges and needn't reach their ends.
There are 2 independent parts, one for each index of `groups`. The reference program is written for one: setup_inputs(seed, part) draws one part's arguments, and reference() takes and returns one part's arrays. A program takes and returns all parts, laid end to end along the dimension named above; an argument that names none is the same for every part. Nothing has to cross between parts.
Inputs may be any that keep to these rules, and one draw needn't show every extreme that they name: `owners`: among the rows of one device, no owner is named by more than 64 slots. `item_last`: hidden states of the items' final tokens.
All inputs are finite; a program needn't handle non-finite values.
Results may differ from the reference program's by a relative error of at most 0.012.
Values may be sent and summed in bfloat16 or wider, within the bound.
A program may use at most 128 MiB of HBM per device.

```python
import math
import jax
import jax.numpy as jnp
import numpy as np
from jax import lax

DI = 2048
DU = 4096
FFW = 6144
HIST_LEN = 128
ITEM_SH = 32
ROWS = 128
HIST = 512
ITEMS = 128
SEQS = 4
CAP = 64
N_SHARD = 4
N_INNER = 4


def draw_item_last(key, part):
    key = jax.random.fold_in(key, 11)
    key_base, key_rows, key_cols = jax.random.split(key, 3)
    row_scale = jnp.exp(jax.random.uniform(key_rows, (ITEMS, 1), minval=0.0, maxval=math.log(10.0)))
    col_scale = jnp.exp(jax.random.uniform(key_cols, (1, DI), minval=0.0, maxval=math.log(10.0))) / 3.0
    base_values = jnp.clip(jax.random.normal(key_base, (ITEMS, DI)), -4.0, 4.0)
    return (base_values * row_scale * col_scale).astype(jnp.bfloat16)


def place_ends(values, own_key, low, largest):
    spot = [jax.random.randint(jax.random.fold_in(own_key, axis), (), 0, length) for axis, length in enumerate(values.shape)]
    widest = values.shape.index(max(values.shape))
    next_to = spot[:widest] + [(spot[widest] + 1) % values.shape[widest]] + spot[widest + 1:]
    return values.at[tuple(spot)].set(low).at[tuple(next_to)].set(largest)


def level_of(key, extent, pieces, low, high):
    gain, own = 1.0, jax.random.fold_in(key, 6)
    for dim, blocks in pieces:
        heights = jnp.exp(jax.random.uniform(jax.random.fold_in(own, dim), (blocks,), jnp.float32, low / len(pieces), high / len(pieces)))
        gain = gain * jnp.repeat(heights, extent[dim] // blocks).reshape([-1 if axis == dim else 1 for axis in range(len(extent))])
    return gain


def shared_out(own_key, own, number, rows, amount, top, limit, lean):
    order = jax.random.permutation(own_key, amount)
    heavy_load, usual = load_shares(amount, rows * top, limit, lean, True), load_shares(amount, rows * top, limit, lean, False)
    places = jnp.arange(amount)

    def named(tallies, rotation):
        used = int((tallies > 0).sum())
        fixed = max(1, used // 4)
        shifted = fixed + (places - fixed + rotation * (used - fixed)) % max(1, amount - fixed)
        return jnp.zeros((amount,), jnp.int32).at[order[jnp.where(places < fixed, places, shifted)]].set(jnp.asarray(tallies, jnp.int32))

    tallies = jnp.where(number % 4 == 0, named(heavy_load, number // 4), named(usual, number - number // 4 - 1))
    mixed = jax.random.permutation(jax.random.fold_in(own, 3), amount)
    source_of, sink = mixed[0:amount // 2 * 2:2], mixed[1:amount // 2 * 2:2]
    margin = jnp.minimum(tallies[source_of] - 1, limit - tallies[sink]) // 2
    margin = jnp.where((source_of == order[0]) | (sink == order[0]) | (tallies[sink] == 0), 0, jnp.maximum(margin, 0))
    shifted = jax.random.randint(jax.random.fold_in(own, 4), (amount // 2,), 0, 1 << 20) % (margin + 1)
    tallies = tallies.at[source_of].add(-shifted).at[sink].add(shifted)
    labels = jnp.searchsorted(jnp.cumsum(tallies), jnp.arange(rows * top), side="right").astype(jnp.int32)
    listing = labels.reshape(top, rows).T
    listing = listing[jax.random.permutation(jax.random.fold_in(own, 1), rows)]
    rotation = jax.random.randint(jax.random.fold_in(own, 2), (rows, 1), 0, top)
    return jnp.take_along_axis(listing, (jnp.arange(top)[None, :] + rotation) % top, axis=1)


def load_shares(count, total, reach, skew, full):
    loads = [(1 << 20) // math.isqrt(grade ** skew) + 1 for grade in range(1, count + 1)]
    largest = reach if full else min(reach, max(-(-total // count), total * loads[0] // sum(loads)))
    least = 1 if total - largest >= count - 1 else 0
    counts, rest = [largest] + [least] * (count - 1), total - largest - least * (count - 1)
    while rest > 0:
        movable = [i for i in range(1, count) if counts[i] < largest] or [i for i in range(1, count) if counts[i] < reach]
        mass, budget = sum([loads[i] for i in movable]), rest
        for i in movable:
            extra = min(reach - counts[i], max(1, budget * loads[i] // mass), rest)
            counts[i] = counts[i] + extra
            rest = rest - extra
    return np.array(counts)


def scatter_about(stream_key, dims, width, bound, pieces=(), kind=jnp.bfloat16):
    result = jax.random.normal(stream_key, dims, jnp.float32) * width
    if len(pieces) > 0:
        result = level_of(stream_key, dims, pieces, -0.22, 0.18) * result
    return jnp.clip(result, min=-bound, max=bound).astype(kind)


def setup_inputs(seed: int = 0, part: int = 0) -> dict:
    streams_of = jax.random.split(jax.random.key(seed), 10)
    own_keys = jax.random.split(jax.random.fold_in(streams_of[9], part), 10)
    item_last = draw_item_last(jax.random.fold_in(jax.random.fold_in(streams_of[9], part), 71), part)
    adapter = scatter_about(streams_of[1], (DI, DU), DI ** -0.5, 0.125, ((1, 4),))
    user_gain = jnp.clip(1.0 + 0.1 * jax.random.normal(streams_of[2], (DU,), jnp.float32), 0.5, 1.5)
    w_gate = scatter_about(streams_of[3], (DU, FFW), DU ** -0.5, 0.09375, ((0, 4), (1, 4)))
    w_up = scatter_about(streams_of[4], (DU, FFW), DU ** -0.5, 0.09375, ((0, 4), (1, 4)))
    owners_keys = jax.random.split(jax.random.fold_in(own_keys[5], 1), HIST // ROWS)
    owners_turns = jax.random.permutation(jax.random.fold_in(own_keys[5], 3), HIST // ROWS)
    owners = jax.vmap(lambda own, number: shared_out(jax.random.fold_in(own_keys[5], 2), own, number, ROWS, N_SHARD, 1, CAP, 2))(owners_keys, owners_turns).reshape((HIST, 1))
    item_rows = place_ends(jax.random.randint(own_keys[6], (HIST,), 0, ITEM_SH), jax.random.fold_in(own_keys[6], 1), 0, ITEM_SH - 1).astype(jnp.int32)
    lengths = place_ends(jax.random.randint(own_keys[7], (SEQS,), HIST_LEN // 4, HIST_LEN + 1), jax.random.fold_in(own_keys[7], 1), HIST_LEN // 4, HIST_LEN).astype(jnp.int32)
    d_hidden = scatter_about(own_keys[8], (HIST, FFW), 1.0, 6.0, ((0, 4), (1, 4)))
    return dict(item_last=item_last, adapter=adapter, user_gain=user_gain, w_gate=w_gate, w_up=w_up, owners=owners, item_rows=item_rows, lengths=lengths, d_hidden=d_hidden)


def reference(item_last, adapter, user_gain, w_gate, w_up, owners, item_rows, lengths, d_hidden):
    embedded = jnp.dot(item_last, adapter, preferred_element_type=jnp.float32).astype(jnp.bfloat16)
    item_ids = (owners[:, 0] * ITEM_SH + item_rows).astype(jnp.int32)
    position = jnp.arange(HIST, dtype=jnp.int32)
    live_rows = position % HIST_LEN < lengths[position // HIST_LEN]
    fetched = embedded[item_ids]
    routed = jnp.where(live_rows[:, None], fetched, jnp.zeros_like(fetched))
    routed_f = routed.astype(jnp.float32)
    inv_rms = lax.rsqrt(lax.optimization_barrier(jnp.mean(routed_f * routed_f, axis=1)) + 1e-05)
    normed = (routed_f * inv_rms[:, None] * user_gain[None, :]).astype(jnp.bfloat16)
    gate_act = jnp.dot(normed, w_gate, preferred_element_type=jnp.float32)
    up_act = jnp.dot(normed, w_up, preferred_element_type=jnp.float32)
    sigmoid_gate = jax.nn.sigmoid(gate_act)
    active = gate_act * sigmoid_gate
    hidden = (active * up_act).astype(jnp.bfloat16)
    grad_f = d_hidden.astype(jnp.float32)
    d_gate = (grad_f * up_act * sigmoid_gate * (1.0 + gate_act * (1.0 - sigmoid_gate))).astype(jnp.bfloat16)
    d_up = (grad_f * active).astype(jnp.bfloat16)
    block_width = FFW // N_INNER
    d_normed = jnp.zeros((HIST, DU), jnp.float32)
    for index in range(N_INNER):
        first = index * block_width
        term_rows = jnp.dot(d_gate[:, first:first + block_width], w_gate[:, first:first + block_width].T, preferred_element_type=jnp.float32)
        term_rows = term_rows + jnp.dot(d_up[:, first:first + block_width], w_up[:, first:first + block_width].T, preferred_element_type=jnp.float32)
        rounded = lax.optimization_barrier(term_rows.astype(jnp.bfloat16))
        d_normed = d_normed + rounded.astype(jnp.float32)
    products = lax.optimization_barrier(jnp.sum(user_gain[None, :] * d_normed * routed_f, axis=1))
    cubed_scale = inv_rms * inv_rms * inv_rms * products / DU
    d_routed = inv_rms[:, None] * user_gain[None, :] * d_normed - routed_f * cubed_scale[:, None]
    d_routed = jnp.where(live_rows[:, None], d_routed, jnp.zeros_like(d_routed)).astype(jnp.bfloat16)
    item_grad = jax.ops.segment_sum(d_routed.astype(jnp.float32), item_ids, num_segments=ITEMS)
    return (hidden, item_grad)
```

```python
import jax
import jax.numpy as jnp
from jax import lax
from jax.sharding import PartitionSpec as P

HIST_LEN = 128


epsilon = 1e-05


def contract_rows(left_side, right_side):
    return lax.dot_general(
        left_side, right_side, (((1,), (1,)), ((), ())), preferred_element_type=jnp.float32
    )


def body(item_last, adapter, user_gain, w_gate, w_up, owners, item_rows, lengths, d_hidden):
    shards = lax.axis_size("shard")
    inner_count = lax.axis_size("inner")
    own_items = item_last.shape[0]
    items = own_items * shards
    row_count = owners.shape[0]
    model_width = user_gain.shape[0]
    own_width = model_width // inner_count
    weight_rows = w_gate.shape[0]
    width = w_gate.shape[1]
    shard_at, inner_at = lax.axis_index("shard"), lax.axis_index("inner")

    ids = owners[:, 0] * own_items + item_rows
    position = jnp.arange(row_count, dtype=jnp.int32) % HIST_LEN
    limit_of = jnp.repeat(lengths, HIST_LEN, total_repeat_length=row_count)
    selector = (
        (ids[:, None] == jnp.arange(items, dtype=jnp.int32)[None, :])
        & (position < limit_of)[:, None]
    ).astype(jnp.bfloat16)

    slot_sums = lax.dot_general(
        selector, d_hidden, (((0,), (0,)), ((), ())), preferred_element_type=jnp.float32
    )
    item_cot = lax.psum(slot_sums.astype(jnp.bfloat16), "shard").astype(jnp.float32)

    embedded = jnp.dot(item_last, adapter, preferred_element_type=jnp.float32).astype(jnp.bfloat16)
    whole_rows = lax.all_gather(embedded, "inner", axis=1, tiled=True)
    block = lax.all_to_all(whole_rows, "shard", split_axis=1, concat_axis=0, tiled=True)
    block_f = block.astype(jnp.float32)
    gain_block = lax.dynamic_slice_in_dim(user_gain, shard_at * weight_rows, weight_rows, 0)
    squares = lax.psum(jnp.sum(block_f * block_f, axis=1), "shard")
    inv_rms = lax.rsqrt(squares / model_width + epsilon)
    scaled = (block_f * gain_block[None, :]).astype(jnp.bfloat16)
    partial_acts = jnp.concatenate(
        [
            jnp.dot(scaled, w_gate, preferred_element_type=jnp.float32).astype(jnp.bfloat16),
            jnp.dot(scaled, w_up, preferred_element_type=jnp.float32).astype(jnp.bfloat16),
        ],
        axis=1,
    )
    acts = lax.psum(partial_acts, "shard").astype(jnp.float32) * inv_rms[:, None]
    gate_act, up_act = acts[:, :width], acts[:, width:]
    sigmoid_gate = jax.nn.sigmoid(gate_act)
    active = gate_act * sigmoid_gate
    item_hidden = (active * up_act).astype(jnp.bfloat16)
    hidden = jnp.dot(selector, item_hidden, preferred_element_type=jnp.float32).astype(jnp.bfloat16)

    d_gate = item_cot * up_act * sigmoid_gate * (1.0 + gate_act * (1.0 - sigmoid_gate))
    d_up = item_cot * active
    dots = lax.psum(jnp.sum(d_gate * gate_act + d_up * up_act, axis=1), "inner")
    terms = contract_rows(d_gate.astype(jnp.bfloat16), w_gate) + contract_rows(
        d_up.astype(jnp.bfloat16), w_up
    )
    own_terms = lax.all_to_all(
        terms.astype(jnp.bfloat16), "shard", split_axis=0, concat_axis=1, tiled=True
    )
    d_normed = lax.psum_scatter(
        own_terms, "inner", scatter_dimension=1, tiled=True
    ).astype(jnp.float32)
    gain_own = lax.dynamic_slice_in_dim(user_gain, inner_at * own_width, own_width, 0)
    inv_own = lax.dynamic_slice_in_dim(inv_rms, shard_at * own_items, own_items, 0)[:, None]
    dots_own = lax.dynamic_slice_in_dim(dots, shard_at * own_items, own_items, 0)[:, None]
    item_grad = inv_own * gain_own[None, :] * d_normed - embedded.astype(jnp.float32) * (
        inv_own * inv_own * dots_own / model_width
    )
    return (hidden, item_grad)


def solution(mesh):
    return jax.shard_map(
        body,
        mesh=mesh,
        in_specs=(
            P(("groups", "shard"), None),
            P(None, "inner"),
            P(),
            P("shard", "inner"),
            P("shard", "inner"),
            P(("groups", "shard"), None),
            P(("groups", "shard")),
            P(("groups", "shard")),
            P(("groups", "shard"), "inner"),
        ),
        out_specs=(P(("groups", "shard"), "inner"), P(("groups", "shard"), "inner")),
        check_vma=False,
    )
```

```python
import functools
import math

import jax
import jax.numpy as jnp
from jax import lax
from jax.experimental import pallas as pl
from jax.experimental.pallas import tpu as pltpu
from jax.sharding import PartitionSpec as P

HIST_LEN = 128


epsilon = 1e-05


def contract_rows(left_side, right_side):
    return lax.dot_general(
        left_side, right_side, (((1,), (1,)), ((), ())), preferred_element_type=jnp.float32
    )


def body(item_last, adapter, user_gain, w_gate, w_up, owners, item_rows, lengths, d_hidden):
    shards = lax.axis_size("shard")
    inner_count = lax.axis_size("inner")
    own_items = item_last.shape[0]
    items = own_items * shards
    row_count = owners.shape[0]
    model_width = user_gain.shape[0]
    own_width = model_width // inner_count
    weight_rows = w_gate.shape[0]
    width = w_gate.shape[1]
    shard_at, inner_at = lax.axis_index("shard"), lax.axis_index("inner")

    ids = owners[:, 0] * own_items + item_rows
    position = jnp.arange(row_count, dtype=jnp.int32) % HIST_LEN
    limit_of = jnp.repeat(lengths, HIST_LEN, total_repeat_length=row_count)
    selector = (
        (ids[:, None] == jnp.arange(items, dtype=jnp.int32)[None, :])
        & (position < limit_of)[:, None]
    ).astype(jnp.bfloat16)

    slot_sums = lax.dot_general(
        selector, d_hidden, (((0,), (0,)), ((), ())), preferred_element_type=jnp.float32
    )
    item_cot = lax.psum(slot_sums.astype(jnp.bfloat16), "shard").astype(jnp.float32)

    embedded = jnp.dot(item_last, adapter, preferred_element_type=jnp.float32).astype(jnp.bfloat16)
    whole_rows = lax.all_gather(embedded, "inner", axis=1, tiled=True)
    block = lax.all_to_all(whole_rows, "shard", split_axis=1, concat_axis=0, tiled=True)
    block_f = block.astype(jnp.float32)
    gain_block = lax.dynamic_slice_in_dim(user_gain, shard_at * weight_rows, weight_rows, 0)
    squares = lax.psum(jnp.sum(block_f * block_f, axis=1), "shard")
    inv_rms = lax.rsqrt(squares / model_width + epsilon)
    scaled = (block_f * gain_block[None, :]).astype(jnp.bfloat16)
    partial_acts = jnp.concatenate(
        [
            jnp.dot(scaled, w_gate, preferred_element_type=jnp.float32).astype(jnp.bfloat16),
            jnp.dot(scaled, w_up, preferred_element_type=jnp.float32).astype(jnp.bfloat16),
        ],
        axis=1,
    )
    acts = lax.psum(partial_acts, "shard").astype(jnp.float32) * inv_rms[:, None]
    gate_act, up_act = acts[:, :width], acts[:, width:]
    sigmoid_gate = jax.nn.sigmoid(gate_act)
    active = gate_act * sigmoid_gate
    item_hidden = (active * up_act).astype(jnp.bfloat16)
    hidden = jnp.dot(selector, item_hidden, preferred_element_type=jnp.float32).astype(jnp.bfloat16)

    d_gate = item_cot * up_act * sigmoid_gate * (1.0 + gate_act * (1.0 - sigmoid_gate))
    d_up = item_cot * active
    dots = lax.psum(jnp.sum(d_gate * gate_act + d_up * up_act, axis=1), "inner")
    terms = contract_rows(d_gate.astype(jnp.bfloat16), w_gate) + contract_rows(
        d_up.astype(jnp.bfloat16), w_up
    )
    own_terms = lax.all_to_all(
        terms.astype(jnp.bfloat16), "shard", split_axis=0, concat_axis=1, tiled=True
    )
    d_normed = lax.psum_scatter(
        own_terms, "inner", scatter_dimension=1, tiled=True
    ).astype(jnp.float32)
    gain_own = lax.dynamic_slice_in_dim(user_gain, inner_at * own_width, own_width, 0)
    inv_own = lax.dynamic_slice_in_dim(inv_rms, shard_at * own_items, own_items, 0)[:, None]
    dots_own = lax.dynamic_slice_in_dim(dots, shard_at * own_items, own_items, 0)[:, None]
    item_grad = inv_own * gain_own[None, :] * d_normed - embedded.astype(jnp.float32) * (
        inv_own * inv_own * dots_own / model_width
    )
    return (hidden, item_grad)


def square_kernel(
    n, ids_ref, item_ref, gain_ref, adapter_hbm, cot_hbm, gate_hbm, up_hbm,
    hidden_ref, grad_ref,
    adapter, cot, w_gate, w_up, own, block, scaled, cot_out, cot_in, act_out, act_in,
    squares, dots, grads_all, hidden_all, terms_out, terms_in,
    load_sem, own_send, own_recv, sq_send, sq_recv, cot_send, cot_recv, act_send, act_recv,
    grads_send, grads_recv, hid_send, hid_recv, dots_send, dots_recv, terms_send, terms_recv,
):
    s, i = lax.axis_index("shard"), lax.axis_index("inner")
    on_diagonal = s == i
    rows, own_width = own.shape
    items, width = cot_out.shape
    depth = block.shape[1]
    model_width = own_width * n

    def shifted(base, by):
        return lax.rem(base + by, n)

    def part(index):
        return pl.ds(pl.multiple_of(index * rows, rows), rows)

    def device(shard, inner):
        return {"shard": shard, "inner": inner}

    def send(src, dst, send_sem, recv_sem, shard, inner):
        return pltpu.make_async_remote_copy(
            src_ref=src, dst_ref=dst, send_sem=send_sem, recv_sem=recv_sem,
            device_id=device(shard, inner), device_id_type=pl.DeviceIdType.MESH,
        )

    loads = [
        pltpu.make_async_copy(src, dst, load_sem.at[k])
        for k, (src, dst) in enumerate(
            [(adapter_hbm, adapter), (cot_hbm, cot), (gate_hbm, w_gate), (up_hbm, w_up)]
        )
    ]
    for load in loads:
        load.start()

    barrier = pltpu.get_barrier_semaphore()

    def greet(shard, inner):
        pl.semaphore_signal(
            barrier, inc=1, device_id=device(shard, inner), device_id_type=pl.DeviceIdType.MESH
        )

    for r in range(1, n):
        greet(shifted(s, r), i)
        greet(s, shifted(i, r))

    @pl.when(jnp.logical_not(on_diagonal))
    def _():
        for r in range(1, n):
            greet(i, shifted(i, r))
            pl.when(shifted(s, r) != i)(functools.partial(greet, shifted(s, r), s))

    loads[0].wait()
    tile = math.gcd(own_width, 256)

    def embed(c, carry):
        at = pl.ds(pl.multiple_of(c * tile, tile), tile)
        own[:, at] = jnp.dot(
            item_ref[...], adapter[:, at], preferred_element_type=jnp.float32
        ).astype(jnp.bfloat16)
        return carry

    lax.fori_loop(0, own_width // tile, embed, 0)
    own_f = own[...].astype(jnp.float32)
    squares[0] = jnp.broadcast_to(jnp.sum(own_f * own_f, axis=1, keepdims=True), (rows, 128))

    @pl.when(on_diagonal)
    def _():
        pl.semaphore_wait(barrier, 2 * (n - 1))

    @pl.when(jnp.logical_not(on_diagonal))
    def _():
        pl.semaphore_wait(barrier, 4 * (n - 1) - 1)

    own_copies = [
        send(own, block.at[part(s)], own_send.at[r], own_recv.at[s], i, shifted(i, r))
        for r in range(n)
    ]
    for copy in own_copies[1:]:
        copy.start()

    @pl.when(jnp.logical_not(on_diagonal))
    def _():
        own_copies[0].start()

    @pl.when(on_diagonal)
    def _():
        block[part(s), :] = own[...]

    sq_copies = [
        send(squares.at[0], squares.at[r], sq_send.at[r - 1], sq_recv.at[r - 1], s, shifted(i, r))
        for r in range(1, n)
    ]
    for copy in sq_copies:
        copy.start()

    chosen = (
        lax.broadcasted_iota(jnp.int32, (items, ids_ref.shape[1]), 0) == ids_ref[...]
    ).astype(jnp.float32).astype(jnp.bfloat16)
    loads[1].wait()
    wide = math.gcd(width, 512)
    for c in range(width // wide):
        at = pl.ds(c * wide, wide)
        cot_out[:, at] = jnp.dot(
            chosen, cot[:, at], preferred_element_type=jnp.float32
        ).astype(jnp.bfloat16)
    cot_copies = [
        send(
            cot_out.at[part(shifted(s, r))], cot_in.at[r - 1],
            cot_send.at[r - 1], cot_recv.at[r - 1], shifted(s, r), i,
        )
        for r in range(1, n)
    ]
    for copy in cot_copies:
        copy.start()

    for r in range(n):
        source = shifted(s, r)
        arrival = send(own, block.at[part(source)], own_send.at[r], own_recv.at[source], source, s)
        if r == 0:
            pl.when(jnp.logical_not(on_diagonal))(arrival.wait_recv)
        else:
            arrival.wait_recv()
    scaled[...] = (block[...].astype(jnp.float32) * gain_ref[pl.ds(s, 1), :]).astype(jnp.bfloat16)
    loads[2].wait()
    loads[3].wait()
    narrow = math.gcd(width, 256)

    def activate(c, carry):
        at = pl.ds(pl.multiple_of(c * narrow, narrow), narrow)
        up_at = pl.ds(pl.multiple_of(c * narrow + width, narrow), narrow)
        act_out[:, at] = jnp.dot(
            scaled[...], w_gate[:, at], preferred_element_type=jnp.float32
        ).astype(jnp.bfloat16)
        act_out[:, up_at] = jnp.dot(
            scaled[...], w_up[:, at], preferred_element_type=jnp.float32
        ).astype(jnp.bfloat16)
        return carry

    lax.fori_loop(0, width // narrow, activate, 0)
    act_copies = [
        send(
            act_out.at[part(shifted(s, r))], act_in.at[r - 1],
            act_send.at[r - 1], act_recv.at[r - 1], shifted(s, r), i,
        )
        for r in range(1, n)
    ]
    for copy in act_copies:
        copy.start()

    for copy in sq_copies:
        copy.wait_recv()
    total = squares[0]
    for r in range(1, n):
        total = total + squares[r]
    inv_rms = lax.rsqrt(total[:, :1] / model_width + epsilon)

    for copy in cot_copies + act_copies:
        copy.wait_recv()
    dot_sum = jnp.zeros((rows, 1), jnp.float32)
    for c in range(width // narrow):
        at, up_at = pl.ds(c * narrow, narrow), pl.ds(c * narrow + width, narrow)

        def whole(out_ref, in_ref, columns):
            value = out_ref[part(s), columns].astype(jnp.float32)
            for r in range(n - 1):
                value = value + in_ref[r, :, columns].astype(jnp.float32)
            return value

        gate_act = whole(act_out, act_in, at) * inv_rms
        up_act = whole(act_out, act_in, up_at) * inv_rms
        item_cot = whole(cot_out, cot_in, at)
        sigmoid_gate = jax.nn.sigmoid(gate_act)
        active = gate_act * sigmoid_gate
        hidden_all[part(s), at] = (active * up_act).astype(jnp.bfloat16)
        d_gate = item_cot * up_act * sigmoid_gate * (1.0 + gate_act * (1.0 - sigmoid_gate))
        d_up = item_cot * active
        grads_all[part(s), at] = d_gate.astype(jnp.bfloat16)
        grads_all[part(s), up_at] = d_up.astype(jnp.bfloat16)
        dot_sum = dot_sum + jnp.sum(d_gate * gate_act + d_up * up_act, axis=1, keepdims=True)
    grads_copies = [
        send(
            grads_all.at[part(s)], grads_all.at[part(s)],
            grads_send.at[r - 1], grads_recv.at[r - 1], shifted(s, r), i,
        )
        for r in range(1, n)
    ]
    hid_copies = [
        send(
            hidden_all.at[part(s)], hidden_all.at[part(s)],
            hid_send.at[r - 1], hid_recv.at[r - 1], shifted(s, r), i,
        )
        for r in range(1, n)
    ]
    for copy in grads_copies:
        copy.start()
    dots[0] = jnp.broadcast_to(dot_sum, (rows, 128))
    dots_copies = [
        send(dots.at[0], dots.at[r], dots_send.at[r - 1], dots_recv.at[r - 1], s, shifted(i, r))
        for r in range(1, n)
    ]
    for copy in dots_copies + hid_copies:
        copy.start()

    for copy in grads_copies:
        copy.wait_recv()
    high = math.gcd(depth, 256)

    def contract(c, carry):
        at = pl.ds(pl.multiple_of(c * high, high), high)
        terms_out[:, at] = (
            contract_rows(grads_all[:, :width], w_gate[at, :])
            + contract_rows(grads_all[:, width:], w_up[at, :])
        ).astype(jnp.bfloat16)
        return carry

    lax.fori_loop(0, depth // high, contract, 0)
    terms_copies = [
        send(
            terms_out.at[part(shifted(s, r))], terms_in.at[i],
            terms_send.at[r], terms_recv.at[i], shifted(s, r), s,
        )
        for r in range(n)
    ]
    for copy in terms_copies[1:]:
        copy.start()

    @pl.when(jnp.logical_not(on_diagonal))
    def _():
        terms_copies[0].start()

    @pl.when(on_diagonal)
    def _():
        terms_in[i] = terms_out[part(s), :]

    for copy in hid_copies:
        copy.wait_recv()
    for c in range(width // wide):
        at = pl.ds(c * wide, wide)
        hidden_ref[:, at] = lax.dot_general(
            chosen, hidden_all[:, at], (((0,), (0,)), ((), ())), preferred_element_type=jnp.float32
        ).astype(jnp.bfloat16)

    for copy in dots_copies:
        copy.wait_recv()
    total = dots[0]
    for r in range(1, n):
        total = total + dots[r]
    shrink = inv_rms * inv_rms * total[:, :1] / model_width
    for r in range(n):
        source = shifted(i, r)
        arrival = send(
            terms_out.at[part(s)], terms_in.at[source], terms_send.at[r], terms_recv.at[source],
            i, source,
        )
        if r == 0:
            pl.when(jnp.logical_not(on_diagonal))(arrival.wait_recv)
        else:
            arrival.wait_recv()
    d_normed = terms_in[0].astype(jnp.float32)
    for r in range(1, n):
        d_normed = d_normed + terms_in[r].astype(jnp.float32)
    grad_ref[...] = inv_rms * gain_ref[pl.ds(i, 1), :] * d_normed - own[...].astype(
        jnp.float32
    ) * shrink

    for copy in (
        sq_copies + cot_copies + act_copies + grads_copies + hid_copies + dots_copies
        + own_copies[1:] + terms_copies[1:]
    ):
        copy.wait_send()

    @pl.when(jnp.logical_not(on_diagonal))
    def _():
        own_copies[0].wait_send()
        terms_copies[0].wait_send()


def square_body(item_last, adapter, user_gain, w_gate, w_up, owners, item_rows, lengths, d_hidden):
    n = lax.axis_size("shard")
    rows, item_width = item_last.shape
    items = rows * n
    row_count = owners.shape[0]
    model_width = user_gain.shape[0]
    own_width = model_width // n
    depth, width = w_gate.shape
    ids = owners.reshape(1, row_count) * rows + item_rows.reshape(1, row_count)
    position = jnp.arange(row_count, dtype=jnp.int32) % HIST_LEN
    limit_of = jnp.repeat(lengths, HIST_LEN, total_repeat_length=row_count)
    ids = jnp.where((position < limit_of)[None, :], ids, -1)
    bf16, f32 = jnp.bfloat16, jnp.float32
    vmem, anywhere = pl.BlockSpec(memory_space=pltpu.VMEM), pl.BlockSpec(memory_space=pl.ANY)
    sems = lambda count: pltpu.SemaphoreType.DMA((count,))
    return pl.pallas_call(
        functools.partial(square_kernel, n),
        out_shape=(
            jax.ShapeDtypeStruct((row_count, width), bf16),
            jax.ShapeDtypeStruct((rows, own_width), f32),
        ),
        in_specs=[vmem] * 3 + [anywhere] * 4,
        out_specs=(vmem, vmem),
        scratch_shapes=[
            pltpu.VMEM((item_width, own_width), bf16),
            pltpu.VMEM((row_count, width), bf16),
            pltpu.VMEM((depth, width), bf16),
            pltpu.VMEM((depth, width), bf16),
            pltpu.VMEM((rows, own_width), bf16),
            pltpu.VMEM((items, depth), bf16),
            pltpu.VMEM((items, depth), bf16),
            pltpu.VMEM((items, width), bf16),
            pltpu.VMEM((n - 1, rows, width), bf16),
            pltpu.VMEM((items, 2 * width), bf16),
            pltpu.VMEM((n - 1, rows, 2 * width), bf16),
            pltpu.VMEM((n, rows, 128), f32),
            pltpu.VMEM((n, rows, 128), f32),
            pltpu.VMEM((items, 2 * width), bf16),
            pltpu.VMEM((items, width), bf16),
            pltpu.VMEM((items, depth), bf16),
            pltpu.VMEM((n, rows, own_width), bf16),
            sems(4),
            sems(n), sems(n),
            sems(n - 1), sems(n - 1),
            sems(n - 1), sems(n - 1),
            sems(n - 1), sems(n - 1),
            sems(n - 1), sems(n - 1),
            sems(n - 1), sems(n - 1),
            sems(n - 1), sems(n - 1),
            sems(n), sems(n),
        ],
        compiler_params=pltpu.CompilerParams(
            collective_id=0, has_side_effects=True, vmem_limit_bytes=58 * 1024 * 1024
        ),
        cost_estimate=pl.CostEstimate(
            flops=8 * items * depth * width, bytes_accessed=4 * depth * width, transcendentals=0
        ),
    )(ids, item_last, user_gain.reshape(n, own_width), adapter, d_hidden, w_gate, w_up)


def solution(mesh):
    square = mesh.shape["shard"] == mesh.shape["inner"]
    return jax.shard_map(
        square_body if square else body,
        mesh=mesh,
        in_specs=(
            P(("groups", "shard"), None),
            P(None, "inner"),
            P(),
            P("shard", "inner"),
            P("shard", "inner"),
            P(("groups", "shard"), None),
            P(("groups", "shard")),
            P(("groups", "shard")),
            P(("groups", "shard"), "inner"),
        ),
        out_specs=(P(("groups", "shard"), "inner"), P(("groups", "shard"), "inner")),
        check_vma=False,
    )
```

```python
import functools
import math

import jax
import jax.numpy as jnp
from jax import lax
from jax.experimental import pallas as pl
from jax.experimental.pallas import tpu as pltpu
from jax.sharding import PartitionSpec as P

HIST_LEN = 128


epsilon = 1e-05


def contract_rows(left_side, right_side):
    return lax.dot_general(
        left_side, right_side, (((1,), (1,)), ((), ())), preferred_element_type=jnp.float32
    )


def body(item_last, adapter, user_gain, w_gate, w_up, owners, item_rows, lengths, d_hidden):
    shards = lax.axis_size("shard")
    inner_count = lax.axis_size("inner")
    own_items = item_last.shape[0]
    items = own_items * shards
    row_count = owners.shape[0]
    model_width = user_gain.shape[0]
    own_width = model_width // inner_count
    weight_rows = w_gate.shape[0]
    width = w_gate.shape[1]
    shard_at, inner_at = lax.axis_index("shard"), lax.axis_index("inner")

    ids = owners[:, 0] * own_items + item_rows
    position = jnp.arange(row_count, dtype=jnp.int32) % HIST_LEN
    limit_of = jnp.repeat(lengths, HIST_LEN, total_repeat_length=row_count)
    selector = (
        (ids[:, None] == jnp.arange(items, dtype=jnp.int32)[None, :])
        & (position < limit_of)[:, None]
    ).astype(jnp.bfloat16)

    slot_sums = lax.dot_general(
        selector, d_hidden, (((0,), (0,)), ((), ())), preferred_element_type=jnp.float32
    )
    item_cot = lax.psum(slot_sums.astype(jnp.bfloat16), "shard").astype(jnp.float32)

    embedded = jnp.dot(item_last, adapter, preferred_element_type=jnp.float32).astype(jnp.bfloat16)
    whole_rows = lax.all_gather(embedded, "inner", axis=1, tiled=True)
    block = lax.all_to_all(whole_rows, "shard", split_axis=1, concat_axis=0, tiled=True)
    block_f = block.astype(jnp.float32)
    gain_block = lax.dynamic_slice_in_dim(user_gain, shard_at * weight_rows, weight_rows, 0)
    squares = lax.psum(jnp.sum(block_f * block_f, axis=1), "shard")
    inv_rms = lax.rsqrt(squares / model_width + epsilon)
    scaled = (block_f * gain_block[None, :]).astype(jnp.bfloat16)
    partial_acts = jnp.concatenate(
        [
            jnp.dot(scaled, w_gate, preferred_element_type=jnp.float32).astype(jnp.bfloat16),
            jnp.dot(scaled, w_up, preferred_element_type=jnp.float32).astype(jnp.bfloat16),
        ],
        axis=1,
    )
    acts = lax.psum(partial_acts, "shard").astype(jnp.float32) * inv_rms[:, None]
    gate_act, up_act = acts[:, :width], acts[:, width:]
    sigmoid_gate = jax.nn.sigmoid(gate_act)
    active = gate_act * sigmoid_gate
    item_hidden = (active * up_act).astype(jnp.bfloat16)
    hidden = jnp.dot(selector, item_hidden, preferred_element_type=jnp.float32).astype(jnp.bfloat16)

    d_gate = item_cot * up_act * sigmoid_gate * (1.0 + gate_act * (1.0 - sigmoid_gate))
    d_up = item_cot * active
    dots = lax.psum(jnp.sum(d_gate * gate_act + d_up * up_act, axis=1), "inner")
    terms = contract_rows(d_gate.astype(jnp.bfloat16), w_gate) + contract_rows(
        d_up.astype(jnp.bfloat16), w_up
    )
    own_terms = lax.all_to_all(
        terms.astype(jnp.bfloat16), "shard", split_axis=0, concat_axis=1, tiled=True
    )
    d_normed = lax.psum_scatter(
        own_terms, "inner", scatter_dimension=1, tiled=True
    ).astype(jnp.float32)
    gain_own = lax.dynamic_slice_in_dim(user_gain, inner_at * own_width, own_width, 0)
    inv_own = lax.dynamic_slice_in_dim(inv_rms, shard_at * own_items, own_items, 0)[:, None]
    dots_own = lax.dynamic_slice_in_dim(dots, shard_at * own_items, own_items, 0)[:, None]
    item_grad = inv_own * gain_own[None, :] * d_normed - embedded.astype(jnp.float32) * (
        inv_own * inv_own * dots_own / model_width
    )
    return (hidden, item_grad)


def line_kernel(
    n, owner_ref, row_ref, length_ref, item_ref, gain_ref, adapter_hbm, cot_hbm, gate_hbm, up_hbm,
    hidden_ref, grad_ref,
    adapter, cot, w_gate, w_up, own, block, scaled, squares, inv_all, dot_fold, dots,
    partial, outer_in, pair, other_in, total, terms, terms_out, terms_in,
    load_sem, own_send, own_recv, sq_send, sq_recv, inv_send, inv_recv, first_send, first_recv,
    second_send, second_recv, third_send, third_recv, dots_send, dots_recv, terms_send, terms_recv,
):
    s, i = lax.axis_index("shard"), lax.axis_index("inner")
    on_diagonal = s == i
    off_diagonal = jnp.logical_not(on_diagonal)
    at_end = jnp.logical_or(s == 0, s == n - 1)
    in_middle = jnp.logical_not(at_end)
    middle = 1 + s // (n - 1)
    outer, other = (s - 1) * (n - 1), n - 1 - s
    rows, own_width = own.shape
    items = block.shape[0]
    depth, width = w_gate.shape
    model_width = own_width * n
    piece = 512
    half = piece // 2
    cot_pieces, act_pieces = width // piece, width // half
    pieces = cot_pieces + act_pieces

    def shifted(base, by):
        return lax.rem(base + by, n)

    def part(index):
        return pl.ds(pl.multiple_of(index * rows, rows), rows)

    def device(shard, inner):
        return {"shard": shard, "inner": inner}

    def send(src, dst, send_sem, recv_sem, shard, inner):
        return pltpu.make_async_remote_copy(
            src_ref=src, dst_ref=dst, send_sem=send_sem, recv_sem=recv_sem,
            device_id=device(shard, inner), device_id_type=pl.DeviceIdType.MESH,
        )

    loads = [
        pltpu.make_async_copy(src, dst, load_sem.at[k])
        for k, (src, dst) in enumerate(
            [(adapter_hbm, adapter), (cot_hbm, cot), (gate_hbm, w_gate), (up_hbm, w_up)]
        )
    ]
    for load in loads:
        load.start()

    barrier = pltpu.get_barrier_semaphore()

    def greet(shard, inner):
        pl.semaphore_signal(
            barrier, inc=1, device_id=device(shard, inner), device_id_type=pl.DeviceIdType.MESH
        )

    for r in range(1, n):
        greet(shifted(s, r), i)
        greet(s, shifted(i, r))

    @pl.when(off_diagonal)
    def _():
        for r in range(1, n):
            greet(i, shifted(i, r))
            pl.when(shifted(s, r) != i)(functools.partial(greet, shifted(s, r), s))

    slots = owner_ref.shape[1]
    position = lax.broadcasted_iota(jnp.int32, (1, slots), 1)
    limit = jnp.zeros((1, slots), jnp.int32)
    for k in range(length_ref.shape[1]):
        limit = jnp.where(
            position >= k * HIST_LEN, length_ref[:, k : k + 1] + k * HIST_LEN, limit
        )
    ids = jnp.where(position < limit, owner_ref[...] * rows + row_ref[...], -1)
    chosen = (
        lax.broadcasted_iota(jnp.int32, (items, slots), 0) == ids
    ).astype(jnp.float32).astype(jnp.bfloat16)

    loads[0].wait()
    tile = math.gcd(own_width, 256)

    def embed(c, carry):
        at = pl.ds(pl.multiple_of(c * tile, tile), tile)
        own[:, at] = jnp.dot(
            item_ref[...], adapter[:, at], preferred_element_type=jnp.float32
        ).astype(jnp.bfloat16)
        return carry

    lax.fori_loop(0, own_width // tile, embed, 0)
    own_f = own[...].astype(jnp.float32)
    squares[0] = jnp.broadcast_to(jnp.sum(own_f * own_f, axis=1, keepdims=True), (rows, 128))

    @pl.when(on_diagonal)
    def _():
        pl.semaphore_wait(barrier, 2 * (n - 1))

    @pl.when(off_diagonal)
    def _():
        pl.semaphore_wait(barrier, 4 * (n - 1) - 1)

    own_copies = [
        send(own, block.at[part(s)], own_send.at[r], own_recv.at[s], i, shifted(i, r))
        for r in range(n)
    ]
    for copy in own_copies[1:]:
        copy.start()

    @pl.when(off_diagonal)
    def _():
        own_copies[0].start()

    @pl.when(on_diagonal)
    def _():
        block[part(s), :] = own[...]

    sq_copies = [
        send(squares.at[0], squares.at[r], sq_send.at[r - 1], sq_recv.at[r - 1], s, shifted(i, r))
        for r in range(1, n)
    ]
    for copy in sq_copies:
        copy.start()

    def columns(k):
        return pl.ds(k * piece, piece)

    def first(k, shard):
        at = columns(k)
        return send(
            partial.at[:, at], outer_in.at[:, at], first_send.at[k], first_recv.at[k], shard, i
        )

    def second(k):
        at = columns(k)
        return send(
            pair.at[:, at], other_in.at[:, at], second_send.at[k], second_recv.at[k], other, i
        )

    def third(k, shard):
        at = columns(k)
        return send(
            total.at[:, at], total.at[:, at], third_send.at[k], third_recv.at[k], shard, i
        )

    def added(left, right, at):
        return (left[:, at].astype(jnp.float32) + right[:, at].astype(jnp.float32)).astype(
            jnp.bfloat16
        )

    def pair_step(k):
        first(k, outer).wait_recv()
        pair[:, columns(k)] = added(partial, outer_in, columns(k))
        second(k).start()

    def total_step(k):
        second(k).wait_recv()
        total[:, columns(k)] = added(pair, other_in, columns(k))
        third(k, outer).start()

    loads[1].wait()
    for k in range(cot_pieces):
        partial[:, columns(k)] = jnp.dot(
            chosen, cot[:, columns(k)], preferred_element_type=jnp.float32
        ).astype(jnp.bfloat16)
        pl.when(at_end)(lambda k=k: first(k, middle).start())

    for copy in sq_copies:
        copy.wait_recv()
    square_sum = squares[0]
    for r in range(1, n):
        square_sum = square_sum + squares[r]
    inv_all[part(s), :] = lax.rsqrt(square_sum / model_width + epsilon)
    inv_copies = [
        send(
            inv_all.at[part(s)], inv_all.at[part(s)], inv_send.at[r - 1], inv_recv.at[r - 1],
            shifted(s, r), i,
        )
        for r in range(1, n)
    ]
    for copy in inv_copies:
        copy.start()

    @pl.when(in_middle)
    def _():
        for k in range(cot_pieces):
            pair_step(k)
            if k > 0:
                total_step(k - 1)

    for r in range(n):
        source = shifted(s, r)
        arrival = send(own, block.at[part(source)], own_send.at[r], own_recv.at[source], source, s)
        if r == 0:
            pl.when(off_diagonal)(arrival.wait_recv)
        else:
            arrival.wait_recv()
    depth_at = pl.ds(pl.multiple_of(s * depth, depth), depth)
    scaled[...] = (block[...].astype(jnp.float32) * gain_ref[:, depth_at]).astype(jnp.bfloat16)
    loads[2].wait()
    loads[3].wait()
    for copy in inv_copies:
        copy.wait_recv()

    def use(c):
        at = pl.ds(c * half, half)
        begin = (cot_pieces + c) * piece
        inv = inv_all[:, :1]
        gate_act = total[:, pl.ds(begin, half)].astype(jnp.float32) * inv
        up_act = total[:, pl.ds(begin + half, half)].astype(jnp.float32) * inv
        item_cot = total[:, at].astype(jnp.float32)
        sigmoid_gate = jax.nn.sigmoid(gate_act)
        active = gate_act * sigmoid_gate
        item_hidden = (active * up_act).astype(jnp.bfloat16)
        d_gate = item_cot * up_act * sigmoid_gate * (1.0 + gate_act * (1.0 - sigmoid_gate))
        d_up = item_cot * active
        product = d_gate * gate_act + d_up * up_act
        fold = product[:, :128]
        for k in range(1, half // 128):
            fold = fold + product[:, k * 128 : (k + 1) * 128]
        dot_fold[...] = fold if c == 0 else dot_fold[...] + fold
        term = contract_rows(d_gate.astype(jnp.bfloat16), w_gate[:, at]) + contract_rows(
            d_up.astype(jnp.bfloat16), w_up[:, at]
        )
        terms[...] = term if c == 0 else terms[...] + term
        hidden_ref[:, at] = lax.dot_general(
            chosen, item_hidden, (((0,), (0,)), ((), ())), preferred_element_type=jnp.float32
        ).astype(jnp.bfloat16)

    for c in range(act_pieces):
        k = cot_pieces + c
        at = pl.ds(c * half, half)
        for offset, weights in ((0, w_gate), (half, w_up)):
            partial[:, pl.ds(k * piece + offset, half)] = jnp.dot(
                scaled[...], weights[:, at], preferred_element_type=jnp.float32
            ).astype(jnp.bfloat16)
        pl.when(at_end)(lambda k=k: first(k, middle).start())

        @pl.when(in_middle)
        def _():
            pair_step(k)
            total_step(k - 1)
            if c > 0:
                use(c - 1)

    @pl.when(in_middle)
    def _():
        total_step(pieces - 1)
        use(act_pieces - 1)

    @pl.when(at_end)
    def _():
        for k in range(cot_pieces):
            third(k, middle).wait_recv()
        for c in range(act_pieces):
            third(cot_pieces + c, middle).wait_recv()
            use(c)

    terms_out[...] = terms[...].astype(jnp.bfloat16)
    terms_copies = [
        send(
            terms_out.at[part(shifted(s, r))], terms_in.at[i],
            terms_send.at[r], terms_recv.at[i], shifted(s, r), s,
        )
        for r in range(n)
    ]
    for copy in terms_copies[1:]:
        copy.start()

    @pl.when(off_diagonal)
    def _():
        terms_copies[0].start()

    @pl.when(on_diagonal)
    def _():
        terms_in[i] = terms_out[part(s), :]

    dots[0] = jnp.broadcast_to(
        jnp.sum(dot_fold[part(s), :], axis=1, keepdims=True), (rows, 128)
    )
    dots_copies = [
        send(dots.at[0], dots.at[r], dots_send.at[r - 1], dots_recv.at[r - 1], s, shifted(i, r))
        for r in range(1, n)
    ]
    for copy in dots_copies:
        copy.start()
    for copy in dots_copies:
        copy.wait_recv()
    dot_sum = dots[0]
    for r in range(1, n):
        dot_sum = dot_sum + dots[r]
    inv_own = inv_all[part(s), :][:, :1]
    shrink = inv_own * inv_own * dot_sum[:, :1] / model_width
    for r in range(n):
        source = shifted(i, r)
        arrival = send(
            terms_out.at[part(s)], terms_in.at[source], terms_send.at[r], terms_recv.at[source],
            i, source,
        )
        if r == 0:
            pl.when(off_diagonal)(arrival.wait_recv)
        else:
            arrival.wait_recv()
    d_normed = terms_in[0].astype(jnp.float32)
    for r in range(1, n):
        d_normed = d_normed + terms_in[r].astype(jnp.float32)
    own_at = pl.ds(pl.multiple_of(i * own_width, own_width), own_width)
    grad_ref[...] = inv_own * gain_ref[:, own_at] * d_normed - own[...].astype(
        jnp.float32
    ) * shrink

    for copy in sq_copies + inv_copies + dots_copies + own_copies[1:] + terms_copies[1:]:
        copy.wait_send()

    @pl.when(off_diagonal)
    def _():
        own_copies[0].wait_send()
        terms_copies[0].wait_send()

    @pl.when(at_end)
    def _():
        for k in range(pieces):
            first(k, middle).wait_send()

    @pl.when(in_middle)
    def _():
        for k in range(pieces):
            second(k).wait_send()
            third(k, outer).wait_send()


def line_body(item_last, adapter, user_gain, w_gate, w_up, owners, item_rows, lengths, d_hidden):
    n = lax.axis_size("shard")
    rows, item_width = item_last.shape
    items = rows * n
    row_count = owners.shape[0]
    own_width = user_gain.shape[0] // n
    depth, width = w_gate.shape
    bf16, f32 = jnp.bfloat16, jnp.float32
    vmem, anywhere = pl.BlockSpec(memory_space=pltpu.VMEM), pl.BlockSpec(memory_space=pl.ANY)
    sems = lambda count: pltpu.SemaphoreType.DMA((count,))
    pieces = width // 512 + width // 256
    sums = pltpu.VMEM((items, 3 * width), bf16)
    return pl.pallas_call(
        functools.partial(line_kernel, n),
        out_shape=(
            jax.ShapeDtypeStruct((row_count, width), bf16),
            jax.ShapeDtypeStruct((rows, own_width), f32),
        ),
        in_specs=[vmem] * 5 + [anywhere] * 4,
        out_specs=(vmem, vmem),
        scratch_shapes=[
            pltpu.VMEM((item_width, own_width), bf16),
            pltpu.VMEM((row_count, width), bf16),
            pltpu.VMEM((depth, width), bf16),
            pltpu.VMEM((depth, width), bf16),
            pltpu.VMEM((rows, own_width), bf16),
            pltpu.VMEM((items, depth), bf16),
            pltpu.VMEM((items, depth), bf16),
            pltpu.VMEM((n, rows, 128), f32),
            pltpu.VMEM((items, 128), f32),
            pltpu.VMEM((items, 128), f32),
            pltpu.VMEM((n, rows, 128), f32),
            sums, sums, sums, sums, sums,
            pltpu.VMEM((items, depth), f32),
            pltpu.VMEM((items, depth), bf16),
            pltpu.VMEM((n, rows, own_width), bf16),
            sems(4),
            sems(n), sems(n),
            sems(n - 1), sems(n - 1),
            sems(n - 1), sems(n - 1),
            sems(pieces), sems(pieces),
            sems(pieces), sems(pieces),
            sems(pieces), sems(pieces),
            sems(n - 1), sems(n - 1),
            sems(n), sems(n),
        ],
        compiler_params=pltpu.CompilerParams(
            collective_id=0, has_side_effects=True, vmem_limit_bytes=58 * 1024 * 1024
        ),
        cost_estimate=pl.CostEstimate(
            flops=8 * items * depth * width, bytes_accessed=4 * depth * width, transcendentals=0
        ),
    )(
        owners.reshape(1, -1), item_rows.reshape(1, -1), lengths.reshape(1, -1),
        item_last, user_gain.reshape(1, -1), adapter, d_hidden, w_gate, w_up,
    )


def solution(mesh):
    on_line = mesh.shape["shard"] == mesh.shape["inner"] == 4
    return jax.shard_map(
        line_body if on_line else body,
        mesh=mesh,
        in_specs=(
            P(("groups", "shard"), None),
            P(None, "inner"),
            P(),
            P("shard", "inner"),
            P("shard", "inner"),
            P(("groups", "shard"), None),
            P(("groups", "shard")),
            P(("groups", "shard")),
            P(("groups", "shard"), "inner"),
        ),
        out_specs=(P(("groups", "shard"), "inner"), P(("groups", "shard"), "inner")),
        check_vma=False,
    )
```

```python
import functools
import math

import jax
import jax.numpy as jnp
from jax import lax
from jax.experimental import pallas as pl
from jax.experimental.pallas import tpu as pltpu
from jax.sharding import PartitionSpec as P

HIST_LEN = 128


epsilon = 1e-05


def contract_rows(left_side, right_side):
    return lax.dot_general(
        left_side, right_side, (((1,), (1,)), ((), ())), preferred_element_type=jnp.float32
    )


def body(item_last, adapter, user_gain, w_gate, w_up, owners, item_rows, lengths, d_hidden):
    shards = lax.axis_size("shard")
    inner_count = lax.axis_size("inner")
    own_items = item_last.shape[0]
    items = own_items * shards
    row_count = owners.shape[0]
    model_width = user_gain.shape[0]
    own_width = model_width // inner_count
    weight_rows = w_gate.shape[0]
    width = w_gate.shape[1]
    shard_at, inner_at = lax.axis_index("shard"), lax.axis_index("inner")

    ids = owners[:, 0] * own_items + item_rows
    position = jnp.arange(row_count, dtype=jnp.int32) % HIST_LEN
    limit_of = jnp.repeat(lengths, HIST_LEN, total_repeat_length=row_count)
    selector = (
        (ids[:, None] == jnp.arange(items, dtype=jnp.int32)[None, :])
        & (position < limit_of)[:, None]
    ).astype(jnp.bfloat16)

    slot_sums = lax.dot_general(
        selector, d_hidden, (((0,), (0,)), ((), ())), preferred_element_type=jnp.float32
    )
    item_cot = lax.psum(slot_sums.astype(jnp.bfloat16), "shard").astype(jnp.float32)

    embedded = jnp.dot(item_last, adapter, preferred_element_type=jnp.float32).astype(jnp.bfloat16)
    whole_rows = lax.all_gather(embedded, "inner", axis=1, tiled=True)
    block = lax.all_to_all(whole_rows, "shard", split_axis=1, concat_axis=0, tiled=True)
    block_f = block.astype(jnp.float32)
    gain_block = lax.dynamic_slice_in_dim(user_gain, shard_at * weight_rows, weight_rows, 0)
    squares = lax.psum(jnp.sum(block_f * block_f, axis=1), "shard")
    inv_rms = lax.rsqrt(squares / model_width + epsilon)
    scaled = (block_f * gain_block[None, :]).astype(jnp.bfloat16)
    partial_acts = jnp.concatenate(
        [
            jnp.dot(scaled, w_gate, preferred_element_type=jnp.float32).astype(jnp.bfloat16),
            jnp.dot(scaled, w_up, preferred_element_type=jnp.float32).astype(jnp.bfloat16),
        ],
        axis=1,
    )
    acts = lax.psum(partial_acts, "shard").astype(jnp.float32) * inv_rms[:, None]
    gate_act, up_act = acts[:, :width], acts[:, width:]
    sigmoid_gate = jax.nn.sigmoid(gate_act)
    active = gate_act * sigmoid_gate
    item_hidden = (active * up_act).astype(jnp.bfloat16)
    hidden = jnp.dot(selector, item_hidden, preferred_element_type=jnp.float32).astype(jnp.bfloat16)

    d_gate = item_cot * up_act * sigmoid_gate * (1.0 + gate_act * (1.0 - sigmoid_gate))
    d_up = item_cot * active
    dots = lax.psum(jnp.sum(d_gate * gate_act + d_up * up_act, axis=1), "inner")
    terms = contract_rows(d_gate.astype(jnp.bfloat16), w_gate) + contract_rows(
        d_up.astype(jnp.bfloat16), w_up
    )
    own_terms = lax.all_to_all(
        terms.astype(jnp.bfloat16), "shard", split_axis=0, concat_axis=1, tiled=True
    )
    d_normed = lax.psum_scatter(
        own_terms, "inner", scatter_dimension=1, tiled=True
    ).astype(jnp.float32)
    gain_own = lax.dynamic_slice_in_dim(user_gain, inner_at * own_width, own_width, 0)
    inv_own = lax.dynamic_slice_in_dim(inv_rms, shard_at * own_items, own_items, 0)[:, None]
    dots_own = lax.dynamic_slice_in_dim(dots, shard_at * own_items, own_items, 0)[:, None]
    item_grad = inv_own * gain_own[None, :] * d_normed - embedded.astype(jnp.float32) * (
        inv_own * inv_own * dots_own / model_width
    )
    return (hidden, item_grad)


def line_kernel(
    n, owner_ref, row_ref, length_ref, item_ref, gain_ref, adapter_hbm, cot_hbm, gate_hbm, up_hbm,
    hidden_ref, grad_ref,
    adapter, cot, w_gate, w_up, own, block, scaled, squares, inv_all, dot_fold, dots,
    partial, outer_in, pair, other_in, total, terms, terms_out, terms_in,
    load_sem, own_send, own_recv, relay_send, sq_send, sq_recv, inv_send, inv_recv, first_send, first_recv,
    second_send, second_recv, third_send, third_recv, dots_send, dots_recv, terms_send, terms_recv,
):
    s, i = lax.axis_index("shard"), lax.axis_index("inner")
    on_diagonal = s == i
    off_diagonal = jnp.logical_not(on_diagonal)
    near = lax.rem(s + i, 2) == 0
    sibling = i + 1 - 2 * lax.rem(i, 2)
    at_end = jnp.logical_or(s == 0, s == n - 1)
    in_middle = jnp.logical_not(at_end)
    middle = 1 + s // (n - 1)
    outer, other = (s - 1) * (n - 1), n - 1 - s
    rows, own_width = own.shape
    items = block.shape[0]
    depth, width = w_gate.shape
    model_width = own_width * n
    piece = 512
    half = piece // 2
    cot_pieces, act_pieces = width // piece, width // half
    pieces = cot_pieces + act_pieces

    def shifted(base, by):
        return lax.rem(base + by, n)

    def part(index):
        return pl.ds(pl.multiple_of(index * rows, rows), rows)

    def device(shard, inner):
        return {"shard": shard, "inner": inner}

    def send(src, dst, send_sem, recv_sem, shard, inner):
        return pltpu.make_async_remote_copy(
            src_ref=src, dst_ref=dst, send_sem=send_sem, recv_sem=recv_sem,
            device_id=device(shard, inner), device_id_type=pl.DeviceIdType.MESH,
        )

    loads = [
        pltpu.make_async_copy(src, dst, load_sem.at[k])
        for k, (src, dst) in enumerate(
            [(cot_hbm, cot), (adapter_hbm, adapter), (gate_hbm, w_gate), (up_hbm, w_up)]
        )
    ]
    for load in loads:
        load.start()

    barrier = pltpu.get_barrier_semaphore()

    def greet(shard, inner):
        pl.semaphore_signal(
            barrier, inc=1, device_id=device(shard, inner), device_id_type=pl.DeviceIdType.MESH
        )

    for r in range(1, n):
        greet(shifted(s, r), i)
        greet(s, shifted(i, r))

    @pl.when(off_diagonal)
    def _():
        for r in range(1, n):
            greet(i, shifted(i, r))
            pl.when(shifted(s, r) != i)(functools.partial(greet, shifted(s, r), s))

    slots = owner_ref.shape[1]
    position = lax.broadcasted_iota(jnp.int32, (1, slots), 1)
    limit = jnp.zeros((1, slots), jnp.int32)
    for k in range(length_ref.shape[1]):
        limit = jnp.where(
            position >= k * HIST_LEN, length_ref[:, k : k + 1] + k * HIST_LEN, limit
        )
    ids = jnp.where(position < limit, owner_ref[...] * rows + row_ref[...], -1)
    chosen = (
        lax.broadcasted_iota(jnp.int32, (items, slots), 0) == ids
    ).astype(jnp.float32).astype(jnp.bfloat16)

    def columns(k):
        return pl.ds(k * piece, piece)

    def first(k, shard):
        at = columns(k)
        return send(
            partial.at[:, at], outer_in.at[:, at], first_send.at[k], first_recv.at[k], shard, i
        )

    def second(k):
        at = columns(k)
        return send(
            pair.at[:, at], other_in.at[:, at], second_send.at[k], second_recv.at[k], other, i
        )

    def third(k, shard):
        at = columns(k)
        return send(
            total.at[:, at], total.at[:, at], third_send.at[k], third_recv.at[k], shard, i
        )

    def added(left, right, at):
        return (left[:, at].astype(jnp.float32) + right[:, at].astype(jnp.float32)).astype(
            jnp.bfloat16
        )

    def pair_step(k):
        first(k, outer).wait_recv()
        pair[:, columns(k)] = added(partial, outer_in, columns(k))
        second(k).start()

    def total_step(k):
        second(k).wait_recv()
        total[:, columns(k)] = added(pair, other_in, columns(k))
        third(k, outer).start()

    loads[0].wait()
    for k in range(cot_pieces):
        partial[:, columns(k)] = jnp.dot(
            chosen, cot[:, columns(k)], preferred_element_type=jnp.float32
        ).astype(jnp.bfloat16)

    @pl.when(on_diagonal)
    def _():
        pl.semaphore_wait(barrier, 2 * (n - 1))

    @pl.when(off_diagonal)
    def _():
        pl.semaphore_wait(barrier, 4 * (n - 1) - 1)

    @pl.when(at_end)
    def _():
        for k in range(cot_pieces):
            first(k, middle).start()

    loads[1].wait()
    tile = math.gcd(own_width, 256)

    def embed(c, carry):
        at = pl.ds(pl.multiple_of(c * tile, tile), tile)
        own[:, at] = jnp.dot(
            item_ref[...], adapter[:, at], preferred_element_type=jnp.float32
        ).astype(jnp.bfloat16)
        return carry

    lax.fori_loop(0, own_width // tile, embed, 0)
    own_f = own[...].astype(jnp.float32)
    squares[0] = jnp.broadcast_to(jnp.sum(own_f * own_f, axis=1, keepdims=True), (rows, 128))

    own_copies = [
        send(own, block.at[part(s)], own_send.at[r // 2], own_recv.at[s], i, shifted(i, r))
        for r in (0, 2)
    ]
    own_copies[1].start()

    @pl.when(off_diagonal)
    def _():
        own_copies[0].start()

    @pl.when(on_diagonal)
    def _():
        block[part(s), :] = own[...]

    sq_copies = [
        send(squares.at[0], squares.at[r], sq_send.at[r - 1], sq_recv.at[r - 1], s, shifted(i, r))
        for r in range(1, n)
    ]
    for copy in sq_copies:
        copy.start()

    for copy in sq_copies:
        copy.wait_recv()
    square_sum = squares[0]
    for r in range(1, n):
        square_sum = square_sum + squares[r]
    inv_all[part(s), :] = lax.rsqrt(square_sum / model_width + epsilon)
    inv_copies = [
        send(
            inv_all.at[part(s)], inv_all.at[part(s)], inv_send.at[r - 1], inv_recv.at[r - 1],
            shifted(s, r), i,
        )
        for r in range(1, n)
    ]
    for copy in inv_copies:
        copy.start()

    @pl.when(in_middle)
    def _():
        pair_step(0)

    relays = [
        send(
            block.at[part(shifted(s, r))], block.at[part(shifted(s, r))],
            relay_send.at[r], own_recv.at[shifted(s, r)], s, sibling,
        )
        for r in range(n)
    ]

    @pl.when(near)
    def _():
        for r in range(n):
            if r == 0:
                pl.when(off_diagonal)(relays[r].wait_recv)
            else:
                relays[r].wait_recv()
            relays[r].start()

    @pl.when(jnp.logical_not(near))
    def _():
        for r in range(n):
            relays[r].wait_recv()

    @pl.when(in_middle)
    def _():
        for k in range(1, cot_pieces):
            pair_step(k)
            total_step(k - 1)

    depth_at = pl.ds(pl.multiple_of(s * depth, depth), depth)
    scaled[...] = (block[...].astype(jnp.float32) * gain_ref[:, depth_at]).astype(jnp.bfloat16)
    loads[2].wait()
    loads[3].wait()
    for copy in inv_copies:
        copy.wait_recv()

    def use(c):
        at = pl.ds(c * half, half)
        begin = (cot_pieces + c) * piece
        inv = inv_all[:, :1]
        gate_act = total[:, pl.ds(begin, half)].astype(jnp.float32) * inv
        up_act = total[:, pl.ds(begin + half, half)].astype(jnp.float32) * inv
        item_cot = total[:, at].astype(jnp.float32)
        sigmoid_gate = jax.nn.sigmoid(gate_act)
        active = gate_act * sigmoid_gate
        item_hidden = (active * up_act).astype(jnp.bfloat16)
        d_gate = item_cot * up_act * sigmoid_gate * (1.0 + gate_act * (1.0 - sigmoid_gate))
        d_up = item_cot * active
        product = d_gate * gate_act + d_up * up_act
        fold = product[:, :128]
        for k in range(1, half // 128):
            fold = fold + product[:, k * 128 : (k + 1) * 128]
        dot_fold[...] = fold if c == 0 else dot_fold[...] + fold
        term = contract_rows(d_gate.astype(jnp.bfloat16), w_gate[:, at]) + contract_rows(
            d_up.astype(jnp.bfloat16), w_up[:, at]
        )
        terms[...] = term if c == 0 else terms[...] + term
        hidden_ref[:, at] = lax.dot_general(
            chosen, item_hidden, (((0,), (0,)), ((), ())), preferred_element_type=jnp.float32
        ).astype(jnp.bfloat16)

    for c in range(act_pieces):
        k = cot_pieces + c
        at = pl.ds(c * half, half)
        for offset, weights in ((0, w_gate), (half, w_up)):
            partial[:, pl.ds(k * piece + offset, half)] = jnp.dot(
                scaled[...], weights[:, at], preferred_element_type=jnp.float32
            ).astype(jnp.bfloat16)
        pl.when(at_end)(lambda k=k: first(k, middle).start())

        @pl.when(in_middle)
        def _():
            pair_step(k)
            total_step(k - 1)
            if c > 0:
                use(c - 1)

    @pl.when(in_middle)
    def _():
        total_step(pieces - 1)
        use(act_pieces - 1)

    @pl.when(at_end)
    def _():
        for k in range(cot_pieces):
            third(k, middle).wait_recv()
        for c in range(act_pieces):
            third(cot_pieces + c, middle).wait_recv()
            use(c)

    dots[0] = jnp.broadcast_to(
        jnp.sum(dot_fold[part(s), :], axis=1, keepdims=True), (rows, 128)
    )
    dots_copies = [
        send(dots.at[0], dots.at[r], dots_send.at[r - 1], dots_recv.at[r - 1], s, shifted(i, r))
        for r in range(1, n)
    ]
    for copy in dots_copies:
        copy.start()
    terms_out[...] = terms[...].astype(jnp.bfloat16)
    terms_copies = [
        send(
            terms_out.at[part(shifted(s, r))], terms_in.at[i],
            terms_send.at[r], terms_recv.at[i], shifted(s, r), s,
        )
        for r in range(n)
    ]
    for copy in terms_copies[1:]:
        copy.start()

    @pl.when(off_diagonal)
    def _():
        terms_copies[0].start()

    @pl.when(on_diagonal)
    def _():
        terms_in[i] = terms_out[part(s), :]

    for copy in dots_copies:
        copy.wait_recv()
    dot_sum = dots[0]
    for r in range(1, n):
        dot_sum = dot_sum + dots[r]
    inv_own = inv_all[part(s), :][:, :1]
    shrink = inv_own * inv_own * dot_sum[:, :1] / model_width
    for r in range(n):
        source = shifted(i, r)
        arrival = send(
            terms_out.at[part(s)], terms_in.at[source], terms_send.at[r], terms_recv.at[source],
            i, source,
        )
        if r == 0:
            pl.when(off_diagonal)(arrival.wait_recv)
        else:
            arrival.wait_recv()
    d_normed = terms_in[0].astype(jnp.float32)
    for r in range(1, n):
        d_normed = d_normed + terms_in[r].astype(jnp.float32)
    own_at = pl.ds(pl.multiple_of(i * own_width, own_width), own_width)
    grad_ref[...] = inv_own * gain_ref[:, own_at] * d_normed - own[...].astype(
        jnp.float32
    ) * shrink

    for copy in sq_copies + inv_copies + dots_copies + own_copies[1:] + terms_copies[1:]:
        copy.wait_send()

    @pl.when(off_diagonal)
    def _():
        own_copies[0].wait_send()
        terms_copies[0].wait_send()

    @pl.when(near)
    def _():
        for copy in relays:
            copy.wait_send()

    @pl.when(at_end)
    def _():
        for k in range(pieces):
            first(k, middle).wait_send()

    @pl.when(in_middle)
    def _():
        for k in range(pieces):
            second(k).wait_send()
            third(k, outer).wait_send()


def hand_over(hidden_in, grad_in, hidden_out, grad_out, sem):
    copies = [
        pltpu.make_async_copy(hidden_in, hidden_out, sem.at[0]),
        pltpu.make_async_copy(grad_in, grad_out, sem.at[1]),
    ]
    for copy in copies:
        copy.start()
    for copy in copies:
        copy.wait()


def line_body(item_last, adapter, user_gain, w_gate, w_up, owners, item_rows, lengths, d_hidden):
    n = lax.axis_size("shard")
    rows, item_width = item_last.shape
    items = rows * n
    row_count = owners.shape[0]
    own_width = user_gain.shape[0] // n
    depth, width = w_gate.shape
    bf16, f32 = jnp.bfloat16, jnp.float32
    vmem, anywhere = pl.BlockSpec(memory_space=pltpu.VMEM), pl.BlockSpec(memory_space=pl.ANY)
    sems = lambda count: pltpu.SemaphoreType.DMA((count,))
    pieces = width // 512 + width // 256
    sums = pltpu.VMEM((items, 3 * width), bf16)
    out_shape = (
        jax.ShapeDtypeStruct((row_count, width), bf16),
        jax.ShapeDtypeStruct((rows, own_width), f32),
    )
    results = pl.pallas_call(
        functools.partial(line_kernel, n),
        out_shape=out_shape,
        in_specs=[vmem] * 5 + [anywhere] * 4,
        out_specs=(vmem, vmem),
        scratch_shapes=[
            pltpu.VMEM((item_width, own_width), bf16),
            pltpu.VMEM((row_count, width), bf16),
            pltpu.VMEM((depth, width), bf16),
            pltpu.VMEM((depth, width), bf16),
            pltpu.VMEM((rows, own_width), bf16),
            pltpu.VMEM((items, depth), bf16),
            pltpu.VMEM((items, depth), bf16),
            pltpu.VMEM((n, rows, 128), f32),
            pltpu.VMEM((items, 128), f32),
            pltpu.VMEM((items, 128), f32),
            pltpu.VMEM((n, rows, 128), f32),
            sums, sums, sums, sums, sums,
            pltpu.VMEM((items, depth), f32),
            pltpu.VMEM((items, depth), bf16),
            pltpu.VMEM((n, rows, own_width), bf16),
            sems(4),
            sems(2), sems(n), sems(n),
            sems(n - 1), sems(n - 1),
            sems(n - 1), sems(n - 1),
            sems(pieces), sems(pieces),
            sems(pieces), sems(pieces),
            sems(pieces), sems(pieces),
            sems(n - 1), sems(n - 1),
            sems(n), sems(n),
        ],
        compiler_params=pltpu.CompilerParams(
            collective_id=0, has_side_effects=True, vmem_limit_bytes=58 * 1024 * 1024
        ),
        cost_estimate=pl.CostEstimate(
            flops=8 * items * depth * width, bytes_accessed=4 * depth * width, transcendentals=0
        ),
    )(
        owners.reshape(1, -1), item_rows.reshape(1, -1), lengths.reshape(1, -1),
        item_last, user_gain.reshape(1, -1), adapter, d_hidden, w_gate, w_up,
    )
    return pl.pallas_call(
        hand_over,
        out_shape=out_shape,
        in_specs=[anywhere] * 2,
        out_specs=(anywhere, anywhere),
        scratch_shapes=[sems(2)],
        compiler_params=pltpu.CompilerParams(vmem_limit_bytes=60 * 1024 * 1024),
    )(*results)


def solution(mesh):
    on_line = mesh.shape["shard"] == mesh.shape["inner"] == 4
    return jax.shard_map(
        line_body if on_line else body,
        mesh=mesh,
        in_specs=(
            P(("groups", "shard"), None),
            P(None, "inner"),
            P(),
            P("shard", "inner"),
            P("shard", "inner"),
            P(("groups", "shard"), None),
            P(("groups", "shard")),
            P(("groups", "shard")),
            P(("groups", "shard"), "inner"),
        ),
        out_specs=(P(("groups", "shard"), "inner"), P(("groups", "shard"), "inner")),
        check_vma=False,
    )
```

```python
import functools
import math

import jax
import jax.numpy as jnp
from jax import lax
from jax.experimental import pallas as pl
from jax.experimental.pallas import tpu as pltpu
from jax.sharding import PartitionSpec as P

HIST_LEN = 128


epsilon = 1e-05


def contract_rows(left_side, right_side):
    return lax.dot_general(
        left_side, right_side, (((1,), (1,)), ((), ())), preferred_element_type=jnp.float32
    )


def body(item_last, adapter, user_gain, w_gate, w_up, owners, item_rows, lengths, d_hidden):
    shards = lax.axis_size("shard")
    inner_count = lax.axis_size("inner")
    own_items = item_last.shape[0]
    items = own_items * shards
    row_count = owners.shape[0]
    model_width = user_gain.shape[0]
    own_width = model_width // inner_count
    weight_rows = w_gate.shape[0]
    width = w_gate.shape[1]
    shard_at, inner_at = lax.axis_index("shard"), lax.axis_index("inner")

    ids = owners[:, 0] * own_items + item_rows
    position = jnp.arange(row_count, dtype=jnp.int32) % HIST_LEN
    limit_of = jnp.repeat(lengths, HIST_LEN, total_repeat_length=row_count)
    selector = (
        (ids[:, None] == jnp.arange(items, dtype=jnp.int32)[None, :])
        & (position < limit_of)[:, None]
    ).astype(jnp.bfloat16)

    slot_sums = lax.dot_general(
        selector, d_hidden, (((0,), (0,)), ((), ())), preferred_element_type=jnp.float32
    )
    item_cot = lax.psum(slot_sums.astype(jnp.bfloat16), "shard").astype(jnp.float32)

    embedded = jnp.dot(item_last, adapter, preferred_element_type=jnp.float32).astype(jnp.bfloat16)
    whole_rows = lax.all_gather(embedded, "inner", axis=1, tiled=True)
    block = lax.all_to_all(whole_rows, "shard", split_axis=1, concat_axis=0, tiled=True)
    block_f = block.astype(jnp.float32)
    gain_block = lax.dynamic_slice_in_dim(user_gain, shard_at * weight_rows, weight_rows, 0)
    squares = lax.psum(jnp.sum(block_f * block_f, axis=1), "shard")
    inv_rms = lax.rsqrt(squares / model_width + epsilon)
    scaled = (block_f * gain_block[None, :]).astype(jnp.bfloat16)
    partial_acts = jnp.concatenate(
        [
            jnp.dot(scaled, w_gate, preferred_element_type=jnp.float32).astype(jnp.bfloat16),
            jnp.dot(scaled, w_up, preferred_element_type=jnp.float32).astype(jnp.bfloat16),
        ],
        axis=1,
    )
    acts = lax.psum(partial_acts, "shard").astype(jnp.float32) * inv_rms[:, None]
    gate_act, up_act = acts[:, :width], acts[:, width:]
    sigmoid_gate = jax.nn.sigmoid(gate_act)
    active = gate_act * sigmoid_gate
    item_hidden = (active * up_act).astype(jnp.bfloat16)
    hidden = jnp.dot(selector, item_hidden, preferred_element_type=jnp.float32).astype(jnp.bfloat16)

    d_gate = item_cot * up_act * sigmoid_gate * (1.0 + gate_act * (1.0 - sigmoid_gate))
    d_up = item_cot * active
    dots = lax.psum(jnp.sum(d_gate * gate_act + d_up * up_act, axis=1), "inner")
    terms = contract_rows(d_gate.astype(jnp.bfloat16), w_gate) + contract_rows(
        d_up.astype(jnp.bfloat16), w_up
    )
    own_terms = lax.all_to_all(
        terms.astype(jnp.bfloat16), "shard", split_axis=0, concat_axis=1, tiled=True
    )
    d_normed = lax.psum_scatter(
        own_terms, "inner", scatter_dimension=1, tiled=True
    ).astype(jnp.float32)
    gain_own = lax.dynamic_slice_in_dim(user_gain, inner_at * own_width, own_width, 0)
    inv_own = lax.dynamic_slice_in_dim(inv_rms, shard_at * own_items, own_items, 0)[:, None]
    dots_own = lax.dynamic_slice_in_dim(dots, shard_at * own_items, own_items, 0)[:, None]
    item_grad = inv_own * gain_own[None, :] * d_normed - embedded.astype(jnp.float32) * (
        inv_own * inv_own * dots_own / model_width
    )
    return (hidden, item_grad)


def line_kernel(
    n, owner_ref, row_ref, length_ref, item_ref, gain_ref, adapter_hbm, cot_hbm, gate_hbm, up_hbm,
    hidden_ref, grad_ref,
    adapter, cot, w_gate, w_up, own, block, scaled, squares, inv_all, dot_fold, dots,
    partial, outer_in, pair, other_in, total, terms, terms_out, terms_in,
    load_sem, own_send, own_recv, relay_send, sq_send, sq_recv, inv_send, inv_recv, first_send, first_recv,
    second_send, second_recv, third_send, third_recv, dots_send, dots_recv, terms_send, terms_recv,
):
    s, i = lax.axis_index("shard"), lax.axis_index("inner")
    on_diagonal = s == i
    off_diagonal = jnp.logical_not(on_diagonal)
    near = lax.rem(s + i, 2) == 0
    sibling = i + 1 - 2 * lax.rem(i, 2)
    at_end = jnp.logical_or(s == 0, s == n - 1)
    in_middle = jnp.logical_not(at_end)
    middle = 1 + s // (n - 1)
    outer, other = (s - 1) * (n - 1), n - 1 - s
    rows, own_width = own.shape
    items = block.shape[0]
    depth, width = w_gate.shape
    model_width = own_width * n
    piece = 512
    half = piece // 2
    cot_pieces, act_pieces = width // piece, width // half
    pieces = cot_pieces + act_pieces

    def shifted(base, by):
        return lax.rem(base + by, n)

    def part(index):
        return pl.ds(pl.multiple_of(index * rows, rows), rows)

    def device(shard, inner):
        return {"shard": shard, "inner": inner}

    def send(src, dst, send_sem, recv_sem, shard, inner):
        return pltpu.make_async_remote_copy(
            src_ref=src, dst_ref=dst, send_sem=send_sem, recv_sem=recv_sem,
            device_id=device(shard, inner), device_id_type=pl.DeviceIdType.MESH,
        )

    loads = [
        pltpu.make_async_copy(src, dst, load_sem.at[k])
        for k, (src, dst) in enumerate(
            [(cot_hbm, cot), (adapter_hbm, adapter), (gate_hbm, w_gate), (up_hbm, w_up)]
        )
    ]
    for load in loads:
        load.start()

    barrier = pltpu.get_barrier_semaphore()

    def greet(shard, inner):
        pl.semaphore_signal(
            barrier, inc=1, device_id=device(shard, inner), device_id_type=pl.DeviceIdType.MESH
        )

    for r in range(1, n):
        greet(shifted(s, r), i)
        greet(s, shifted(i, r))

    @pl.when(off_diagonal)
    def _():
        for r in range(1, n):
            greet(i, shifted(i, r))
            pl.when(shifted(s, r) != i)(functools.partial(greet, shifted(s, r), s))

    slots = owner_ref.shape[1]
    position = lax.broadcasted_iota(jnp.int32, (1, slots), 1)
    limit = jnp.zeros((1, slots), jnp.int32)
    for k in range(length_ref.shape[1]):
        limit = jnp.where(
            position >= k * HIST_LEN, length_ref[:, k : k + 1] + k * HIST_LEN, limit
        )
    ids = jnp.where(position < limit, owner_ref[...] * rows + row_ref[...], -1)
    chosen = (
        lax.broadcasted_iota(jnp.int32, (items, slots), 0) == ids
    ).astype(jnp.float32).astype(jnp.bfloat16)

    def columns(k):
        return pl.ds(k * piece, piece)

    def first(k, shard):
        at = columns(k)
        return send(
            partial.at[:, at], outer_in.at[:, at], first_send.at[k], first_recv.at[k], shard, i
        )

    def second(k):
        at = columns(k)
        return send(
            pair.at[:, at], other_in.at[:, at], second_send.at[k], second_recv.at[k], other, i
        )

    def third(k, shard):
        at = columns(k)
        return send(
            total.at[:, at], total.at[:, at], third_send.at[k], third_recv.at[k], shard, i
        )

    def added(left, right, at):
        return (left[:, at].astype(jnp.float32) + right[:, at].astype(jnp.float32)).astype(
            jnp.bfloat16
        )

    def pair_step(k):
        first(k, outer).wait_recv()
        pair[:, columns(k)] = added(partial, outer_in, columns(k))
        second(k).start()

    def total_step(k):
        second(k).wait_recv()
        total[:, columns(k)] = added(pair, other_in, columns(k))
        third(k, outer).start()

    loads[0].wait()
    for k in range(cot_pieces):
        partial[:, columns(k)] = jnp.dot(
            chosen, cot[:, columns(k)], preferred_element_type=jnp.float32
        ).astype(jnp.bfloat16)

    @pl.when(on_diagonal)
    def _():
        pl.semaphore_wait(barrier, 2 * (n - 1))

    @pl.when(off_diagonal)
    def _():
        pl.semaphore_wait(barrier, 4 * (n - 1) - 1)

    @pl.when(at_end)
    def _():
        for k in range(cot_pieces):
            first(k, middle).start()

    loads[1].wait()
    tile = math.gcd(own_width, 256)

    def embed(c, carry):
        at = pl.ds(pl.multiple_of(c * tile, tile), tile)
        own[:, at] = jnp.dot(
            item_ref[...], adapter[:, at], preferred_element_type=jnp.float32
        ).astype(jnp.bfloat16)
        return carry

    lax.fori_loop(0, own_width // tile, embed, 0)
    own_f = own[...].astype(jnp.float32)
    squares[0] = jnp.broadcast_to(jnp.sum(own_f * own_f, axis=1, keepdims=True), (rows, 128))

    own_copies = [
        send(own, block.at[part(s)], own_send.at[r // 2], own_recv.at[s], i, shifted(i, r))
        for r in (0, 2)
    ]
    own_copies[1].start()

    @pl.when(off_diagonal)
    def _():
        own_copies[0].start()

    @pl.when(on_diagonal)
    def _():
        block[part(s), :] = own[...]

    sq_copies = [
        send(squares.at[0], squares.at[r], sq_send.at[r - 1], sq_recv.at[r - 1], s, shifted(i, r))
        for r in range(1, n)
    ]
    for copy in sq_copies:
        copy.start()

    for copy in sq_copies:
        copy.wait_recv()
    square_sum = squares[0]
    for r in range(1, n):
        square_sum = square_sum + squares[r]
    inv_all[part(s), :] = lax.rsqrt(square_sum / model_width + epsilon)
    inv_copies = [
        send(
            inv_all.at[part(s)], inv_all.at[part(s)], inv_send.at[r - 1], inv_recv.at[r - 1],
            shifted(s, r), i,
        )
        for r in range(1, n)
    ]
    for copy in inv_copies:
        copy.start()

    @pl.when(in_middle)
    def _():
        pair_step(0)

    relays = [
        send(
            block.at[part(shifted(s, r))], block.at[part(shifted(s, r))],
            relay_send.at[r], own_recv.at[shifted(s, r)], s, sibling,
        )
        for r in range(n)
    ]

    @pl.when(near)
    def _():
        for r in range(n):
            if r == 0:
                pl.when(off_diagonal)(relays[r].wait_recv)
            else:
                relays[r].wait_recv()
            relays[r].start()

    @pl.when(jnp.logical_not(near))
    def _():
        for r in range(n):
            relays[r].wait_recv()

    @pl.when(in_middle)
    def _():
        for k in range(1, cot_pieces):
            pair_step(k)
            total_step(k - 1)

    depth_at = pl.ds(pl.multiple_of(s * depth, depth), depth)
    scaled[...] = (block[...].astype(jnp.float32) * gain_ref[:, depth_at]).astype(jnp.bfloat16)
    loads[2].wait()
    loads[3].wait()
    for copy in inv_copies:
        copy.wait_recv()

    def use(c):
        at = pl.ds(c * half, half)
        begin = (cot_pieces + c) * piece
        inv = inv_all[:, :1]
        gate_act = total[:, pl.ds(begin, half)].astype(jnp.float32) * inv
        up_act = total[:, pl.ds(begin + half, half)].astype(jnp.float32) * inv
        item_cot = total[:, at].astype(jnp.float32)
        sigmoid_gate = jax.nn.sigmoid(gate_act)
        active = gate_act * sigmoid_gate
        item_hidden = (active * up_act).astype(jnp.bfloat16)
        d_gate = item_cot * up_act * sigmoid_gate * (1.0 + gate_act * (1.0 - sigmoid_gate))
        d_up = item_cot * active
        product = d_gate * gate_act + d_up * up_act
        fold = product[:, :128]
        for k in range(1, half // 128):
            fold = fold + product[:, k * 128 : (k + 1) * 128]
        dot_fold[...] = fold if c == 0 else dot_fold[...] + fold
        term = contract_rows(d_gate.astype(jnp.bfloat16), w_gate[:, at]) + contract_rows(
            d_up.astype(jnp.bfloat16), w_up[:, at]
        )
        terms[...] = term if c == 0 else terms[...] + term
        hidden_ref[:, at] = lax.dot_general(
            chosen, item_hidden, (((0,), (0,)), ((), ())), preferred_element_type=jnp.float32
        ).astype(jnp.bfloat16)

    for c in range(act_pieces):
        k = cot_pieces + c
        at = pl.ds(c * half, half)
        for offset, weights in ((0, w_gate), (half, w_up)):
            partial[:, pl.ds(k * piece + offset, half)] = jnp.dot(
                scaled[...], weights[:, at], preferred_element_type=jnp.float32
            ).astype(jnp.bfloat16)
        pl.when(at_end)(lambda k=k: first(k, middle).start())

        @pl.when(in_middle)
        def _():
            pair_step(k)
            total_step(k - 1)
            if c > 0:
                use(c - 1)

    @pl.when(in_middle)
    def _():
        total_step(pieces - 1)
        use(act_pieces - 1)

    @pl.when(at_end)
    def _():
        for k in range(cot_pieces):
            third(k, middle).wait_recv()
        for c in range(act_pieces):
            third(cot_pieces + c, middle).wait_recv()
            use(c)

    dots[0] = jnp.broadcast_to(
        jnp.sum(dot_fold[part(s), :], axis=1, keepdims=True), (rows, 128)
    )
    dots_copies = [
        send(dots.at[0], dots.at[r], dots_send.at[r - 1], dots_recv.at[r - 1], s, shifted(i, r))
        for r in range(1, n)
    ]
    for copy in dots_copies:
        copy.start()
    terms_out[...] = terms[...].astype(jnp.bfloat16)
    terms_copies = [
        send(
            terms_out.at[part(shifted(s, r))], terms_in.at[i],
            terms_send.at[r], terms_recv.at[i], shifted(s, r), s,
        )
        for r in range(n)
    ]
    for copy in terms_copies[1:]:
        copy.start()

    @pl.when(off_diagonal)
    def _():
        terms_copies[0].start()

    @pl.when(on_diagonal)
    def _():
        terms_in[i] = terms_out[part(s), :]

    for copy in dots_copies:
        copy.wait_recv()
    dot_sum = dots[0]
    for r in range(1, n):
        dot_sum = dot_sum + dots[r]
    inv_own = inv_all[part(s), :][:, :1]
    shrink = inv_own * inv_own * dot_sum[:, :1] / model_width
    for r in range(n):
        source = shifted(i, r)
        arrival = send(
            terms_out.at[part(s)], terms_in.at[source], terms_send.at[r], terms_recv.at[source],
            i, source,
        )
        if r == 0:
            pl.when(off_diagonal)(arrival.wait_recv)
        else:
            arrival.wait_recv()
    d_normed = terms_in[0].astype(jnp.float32)
    for r in range(1, n):
        d_normed = d_normed + terms_in[r].astype(jnp.float32)
    own_at = pl.ds(pl.multiple_of(i * own_width, own_width), own_width)
    grad_ref[...] = inv_own * gain_ref[:, own_at] * d_normed - own[...].astype(
        jnp.float32
    ) * shrink

    for copy in sq_copies + inv_copies + dots_copies + own_copies[1:] + terms_copies[1:]:
        copy.wait_send()

    @pl.when(off_diagonal)
    def _():
        own_copies[0].wait_send()
        terms_copies[0].wait_send()

    @pl.when(near)
    def _():
        for copy in relays:
            copy.wait_send()

    @pl.when(at_end)
    def _():
        for k in range(pieces):
            first(k, middle).wait_send()

    @pl.when(in_middle)
    def _():
        for k in range(pieces):
            second(k).wait_send()
            third(k, outer).wait_send()


def hand_over(hidden_in, grad_in, hidden_out, grad_out):
    hidden_out[...] = hidden_in[...]
    grad_out[...] = grad_in[...]


def line_body(item_last, adapter, user_gain, w_gate, w_up, owners, item_rows, lengths, d_hidden):
    n = lax.axis_size("shard")
    rows, item_width = item_last.shape
    items = rows * n
    row_count = owners.shape[0]
    own_width = user_gain.shape[0] // n
    depth, width = w_gate.shape
    bf16, f32 = jnp.bfloat16, jnp.float32
    vmem, anywhere = pl.BlockSpec(memory_space=pltpu.VMEM), pl.BlockSpec(memory_space=pl.ANY)
    sems = lambda count: pltpu.SemaphoreType.DMA((count,))
    pieces = width // 512 + width // 256
    sums = pltpu.VMEM((items, 3 * width), bf16)
    out_shape = (
        jax.ShapeDtypeStruct((row_count, width), bf16),
        jax.ShapeDtypeStruct((rows, own_width), f32),
    )
    results = pl.pallas_call(
        functools.partial(line_kernel, n),
        out_shape=out_shape,
        in_specs=[vmem] * 5 + [anywhere] * 4,
        out_specs=(vmem, vmem),
        scratch_shapes=[
            pltpu.VMEM((item_width, own_width), bf16),
            pltpu.VMEM((row_count, width), bf16),
            pltpu.VMEM((depth, width), bf16),
            pltpu.VMEM((depth, width), bf16),
            pltpu.VMEM((rows, own_width), bf16),
            pltpu.VMEM((items, depth), bf16),
            pltpu.VMEM((items, depth), bf16),
            pltpu.VMEM((n, rows, 128), f32),
            pltpu.VMEM((items, 128), f32),
            pltpu.VMEM((items, 128), f32),
            pltpu.VMEM((n, rows, 128), f32),
            sums, sums, sums, sums, sums,
            pltpu.VMEM((items, depth), f32),
            pltpu.VMEM((items, depth), bf16),
            pltpu.VMEM((n, rows, own_width), bf16),
            sems(4),
            sems(2), sems(n), sems(n),
            sems(n - 1), sems(n - 1),
            sems(n - 1), sems(n - 1),
            sems(pieces), sems(pieces),
            sems(pieces), sems(pieces),
            sems(pieces), sems(pieces),
            sems(n - 1), sems(n - 1),
            sems(n), sems(n),
        ],
        compiler_params=pltpu.CompilerParams(
            collective_id=0, has_side_effects=True, vmem_limit_bytes=58 * 1024 * 1024
        ),
        cost_estimate=pl.CostEstimate(
            flops=8 * items * depth * width, bytes_accessed=4 * depth * width, transcendentals=0
        ),
    )(
        owners.reshape(1, -1), item_rows.reshape(1, -1), lengths.reshape(1, -1),
        item_last, user_gain.reshape(1, -1), adapter, d_hidden, w_gate, w_up,
    )
    return pl.pallas_call(
        hand_over,
        out_shape=out_shape,
        in_specs=[vmem] * 2,
        out_specs=(vmem, vmem),
    )(*results)


def solution(mesh):
    on_line = mesh.shape["shard"] == mesh.shape["inner"] == 4
    return jax.shard_map(
        line_body if on_line else body,
        mesh=mesh,
        in_specs=(
            P(("groups", "shard"), None),
            P(None, "inner"),
            P(),
            P("shard", "inner"),
            P("shard", "inner"),
            P(("groups", "shard"), None),
            P(("groups", "shard")),
            P(("groups", "shard")),
            P(("groups", "shard"), "inner"),
        ),
        out_specs=(P(("groups", "shard"), "inner"), P(("groups", "shard"), "inner")),
        check_vma=False,
    )
```
